32 devices in a mesh: ctx: 16 (over z, x, core), chan: 2 (over y).
Axes of the slice: x: 2, y: 2, z: 4, core: 2. Of those that a mesh axis runs over, the one named last changes fastest.
Arguments:
- raw_query: bfloat16 [4096, 4096], P('ctx', 'chan'), may hold values from -6 to 6
- raw_key: bfloat16 [4096, 4096], P('ctx', 'chan'), may hold values from -6 to 6
- raw_value: bfloat16 [4096, 4096], P('ctx', 'chan'), may hold values from -6 to 6
- short_filter: float32 [3, 3, 4096], P(None, None, 'chan'), may hold values from -3 to 3
- long_filter: float32 [4096, 4096], P('ctx', 'chan'), may hold values from -6 to 6
- skip: float32 [4096], P('chan'), may hold values from -1 to 1
- w_out: bfloat16 [4096, 8192], P('chan'), may hold values from -0.125 to 0.125
Outputs:
- output: bfloat16 [4096, 8192], P('ctx', 'chan')
The draws below stay inside these ranges and needn't reach their ends.
All inputs are finite; a program needn't handle non-finite values.
Results may differ from the reference program's by a relative error of at most 0.005.
Values may be sent and summed in bfloat16 or wider, within the bound.
A program may use at most 256 MiB of HBM per device.

```python
import jax
import jax.numpy as jnp
from jax import lax

D = 8192
C = 4096
TOK_DEV = 256
SEQ = 4096
N_CTX = 16


def decay_energy(rate_sum):
    return jnp.expm1(-rate_sum * SEQ) / jnp.expm1(-rate_sum)


def draw_long_filter(key, part):
    key = jax.random.fold_in(key, 7)
    rate_key, slow_key, share_key, noise_key = jax.random.split(key, 4)
    fast_rates = jnp.exp(jax.random.uniform(rate_key, (C,), jnp.float32, jnp.log(0.1 / SEQ), jnp.log(1.0 / 30.0)))
    slow_rates = jnp.exp(jax.random.uniform(slow_key, (C,), jnp.float32, jnp.log(0.1 / SEQ), jnp.log(1.0 / SEQ)))
    shares = jax.random.uniform(share_key, (C,), jnp.float32, 0.15, 0.4)
    fluctuation = jnp.clip(jax.random.normal(noise_key, (SEQ, C), jnp.float32), -6.0, 6.0)
    positions = jnp.arange(SEQ, dtype=jnp.float32)[:, None]
    fast_amp = jnp.sqrt(1.0 - shares) / jnp.sqrt(decay_energy(2.0 * fast_rates))
    slow_amp = jnp.sqrt(shares) / jnp.sqrt(decay_energy(2.0 * slow_rates))
    combined = 1.0 + 2.0 * fast_amp * slow_amp * decay_energy(fast_rates + slow_rates)
    envelope = fast_amp * jnp.exp(-fast_rates * positions) + slow_amp * jnp.exp(-slow_rates * positions)
    return fluctuation * envelope / jnp.sqrt(combined)


def strengthened(array, key, source, target, blocks, factor):
    def block_of(dim):
        return (jnp.arange(array.shape[dim]) // (array.shape[dim] // blocks)).reshape((-1,) + (1,) * (array.ndim - 1 - dim))

    near = jax.random.permutation(key, blocks)[block_of(target)]
    far = (block_of(target) + blocks // 2) % blocks
    return jnp.where((block_of(source) == near) | (block_of(source) == far), factor * array, array)


def block_levels(rng, extent, shards, least, largest):
    gain, own = 1.0, jax.random.fold_in(rng, 6)
    for dim, blocks in shards:
        draws = jnp.exp(jax.random.uniform(jax.random.fold_in(own, dim), (blocks,), jnp.float32, least / len(shards), largest / len(shards)))
        gain = gain * jnp.repeat(draws, extent[dim] // blocks).reshape([-1 if axis == dim else 1 for axis in range(len(extent))])
    return gain


def gaussian(rng, dims, width, reach, cuts=(), kind=jnp.bfloat16):
    entries = jax.random.normal(rng, dims, jnp.float32) * width
    if len(cuts) > 0:
        entries = block_levels(rng, dims, cuts, -0.22, 0.18) * entries
    return jnp.clip(entries, min=-reach, max=reach).astype(kind)


def gaussian_with(stream_key, shape, width, reach, cuts, heavy, held_as=jnp.bfloat16):
    array = width * jax.random.normal(stream_key, shape, jnp.float32)
    if cuts:
        array = array * block_levels(stream_key, shape, cuts, -0.22, 0.18)
    return jnp.clip(strengthened(array, jax.random.fold_in(stream_key, 3), *heavy), -reach, reach).astype(held_as)


def setup_inputs(seed: int = 0) -> dict:
    streams_of = jax.random.split(jax.random.key(seed), 8)
    raw_query = gaussian(streams_of[0], (SEQ, C), 1.0, 6.0, ((0, 16), (1, 2)))
    raw_key = gaussian(streams_of[1], (SEQ, C), 1.0, 6.0, ((0, 16), (1, 2)))
    raw_value = gaussian(streams_of[2], (SEQ, C), 1.0, 6.0, ((0, 16), (1, 2)))
    short_filter = gaussian(streams_of[3], (3, 3, C), 0.6, 3.0, ((2, 2),), jnp.float32)
    long_filter = draw_long_filter(jax.random.fold_in(streams_of[7], 71), 0)
    skip = jnp.clip(jax.random.uniform(streams_of[5], (C,), jnp.float32, -1.0, 1.0) * block_levels(streams_of[5], (C,), ((0, 2),), -0.4, 0.0), -1.0, 1.0)
    w_out = gaussian_with(streams_of[6], (C, D), C ** -0.5, 0.125, ((0, 2),), (0, 1, 2, 2.0))
    return {"raw_query": raw_query, "raw_key": raw_key, "raw_value": raw_value, "short_filter": short_filter, "long_filter": long_filter, "skip": skip, "w_out": w_out}


def reference(raw_query, raw_key, raw_value, short_filter, long_filter, skip, w_out):
    filtered = []
    for branch, raw in enumerate((raw_query, raw_key, raw_value)):
        padded = jnp.concatenate([jnp.zeros((2, C), jnp.float32), raw.astype(jnp.float32)], axis=0)
        filtered.append(short_filter[branch, 0] * padded[2:] + short_filter[branch, 1] * padded[1:-1] + short_filter[branch, 2] * padded[:-2])
    queries, key_rows, value_rows = filtered
    mixed = key_rows * value_rows
    length = mixed.shape[0]
    spectrum = jnp.fft.rfft(mixed, n=2 * length, axis=0) * jnp.fft.rfft(long_filter, n=2 * length, axis=0)
    convolved = jnp.fft.irfft(spectrum, n=2 * length, axis=0)[:length]
    gated = (queries * (convolved + skip * mixed)).astype(jnp.bfloat16)
    blocks = gated.reshape(N_CTX, TOK_DEV, C)
    result = lax.map(lambda row_block: jnp.dot(row_block, w_out, preferred_element_type=jnp.float32).astype(jnp.bfloat16), blocks)
    return result.reshape(length, D)
```

```python
import math

import jax
import jax.numpy as jnp
import numpy as np
from jax import lax
from jax.sharding import PartitionSpec as P

three_pass = lax.Precision.HIGH


def passed_along(value, axis, steps):
    count = lax.axis_size(axis)
    first, last = (max(0, -steps), min(count, count - steps))
    return lax.ppermute(value, axis, [(source, source + steps) for source in range(first, last)])


def outer_table(outer):
    half = outer // 2
    angle = 2.0 * np.pi / outer * (np.outer(np.arange(half + 1), np.arange(half)) % outer)
    return np.concatenate([np.cos(angle), -np.sin(angle)], axis=0).astype(np.float32)


def inner_tables(outer, inner):
    total = outer * inner
    k1 = np.arange(outer // 2 + 1)[:, None, None]
    k2 = np.arange(inner)[None, :, None]
    n2 = np.arange(inner)[None, None, :]
    angle = 2.0 * np.pi / total * (n2 * (k1 + outer * k2) % total)
    c, s = np.cos(angle), np.sin(angle)
    top = np.concatenate([c, s], axis=2)
    low = np.concatenate([-s, c], axis=2)
    return np.concatenate([top, low], axis=1).astype(np.float32)


def local_convolution(signal, kernel):
    length, width = signal.shape
    inner = 128
    outer = 2 * length // inner
    half = outer // 2
    first = jnp.asarray(outer_table(outer))
    second = jnp.asarray(inner_tables(outer, inner))
    both = jnp.concatenate([signal, kernel], axis=1).astype(jnp.float32)
    both = both.reshape(half, inner, 2 * width)
    spread = jnp.einsum("kn,nmc->kmc", first, both, precision=three_pass)
    spread = jnp.concatenate([spread[: half + 1], spread[half + 1 :]], axis=1)
    spectrum = jnp.einsum("kpq,kqc->kpc", second, spread, precision=three_pass)
    real, imag = spectrum[:, :inner], spectrum[:, inner:]
    xr, hr = real[..., :width], real[..., width:]
    xi, hi = imag[..., :width], imag[..., width:]
    product = jnp.concatenate([xr * hr - xi * hi, xr * hi + xi * hr], axis=1)
    back = jnp.einsum("kpq,kpc->kqc", second, product, precision=three_pass)
    stacked = jnp.concatenate([back[:, :inner], back[:, inner:]], axis=0)
    weight = np.full((half + 1,), 2.0)
    weight[0] = weight[-1] = 1.0
    scale = np.concatenate([weight, weight])[:, None] / (2 * length)
    last = jnp.asarray((outer_table(outer) * scale).astype(np.float32))
    rows = jnp.einsum("kn,kmc->nmc", last, stacked, precision=three_pass)
    return rows.reshape(length, width)


def local(raw_query, raw_key, raw_value, short_filter, long_filter, skip, w_out):
    raw_list = [raw.astype(jnp.float32) for raw in (raw_query, raw_key, raw_value)]
    width = raw_list[0].shape[1]
    tail_rows = jnp.concatenate([raw_list[0][-2:], raw_list[1][-2:], raw_list[2][-2:]], axis=1)
    before = passed_along(tail_rows, "ctx", 1)
    filtered = []
    for branch in range(3):
        padded = jnp.concatenate(
            [before[:, branch * width : (branch + 1) * width], raw_list[branch]], axis=0
        )
        filtered.append(
            short_filter[branch, 0] * padded[2:]
            + short_filter[branch, 1] * padded[1:-1]
            + short_filter[branch, 2] * padded[:-2]
        )
    queries, key_rows, value_rows = filtered
    mixed = key_rows * value_rows
    kernel = lax.all_to_all(
        long_filter.astype(jnp.bfloat16), "ctx", split_axis=1, concat_axis=0, tiled=True
    )
    signal = lax.all_to_all(
        mixed.astype(jnp.bfloat16), "ctx", split_axis=1, concat_axis=0, tiled=True
    )
    convolved = local_convolution(signal, kernel).astype(jnp.bfloat16)
    convolved = lax.all_to_all(convolved, "ctx", split_axis=0, concat_axis=1, tiled=True)
    gated = (queries * (convolved.astype(jnp.float32) + skip * mixed)).astype(jnp.bfloat16)
    count = lax.axis_size("chan")
    me = lax.axis_index("chan")
    features = w_out.shape[1] // count

    def share(owner):
        columns = lax.dynamic_slice_in_dim(w_out, owner * features, features, axis=1)
        return jnp.dot(gated, columns, preferred_element_type=jnp.float32)

    arrived = []
    for step in range(1, count):
        pairs = [(source, (source + step) % count) for source in range(count)]
        arrived.append(lax.ppermute(share((me + step) % count).astype(jnp.bfloat16), "chan", pairs))
    summed = share(me)
    for part in arrived:
        summed = summed + part.astype(jnp.float32)
    return summed.astype(jnp.bfloat16)


def solution(mesh):
    in_specs = (
        P("ctx", "chan"),
        P("ctx", "chan"),
        P("ctx", "chan"),
        P(None, None, "chan"),
        P("ctx", "chan"),
        P("chan"),
        P("chan", None),
    )
    out_specs = P("ctx", "chan")
    return jax.shard_map(local, mesh=mesh, in_specs=in_specs, out_specs=out_specs, check_vma=False)
```

```python
import functools
import math

import jax
import jax.numpy as jnp
import numpy as np
from jax import lax
from jax.experimental import pallas as pl
from jax.experimental.pallas import tpu as pltpu
from jax.sharding import PartitionSpec as P

three_pass = lax.Precision.HIGH


def passed_along(value, axis, steps):
    count = lax.axis_size(axis)
    first, last = (max(0, -steps), min(count, count - steps))
    return lax.ppermute(value, axis, [(source, source + steps) for source in range(first, last)])


def outer_table(outer):
    half = outer // 2
    angle = 2.0 * np.pi / outer * (np.outer(np.arange(half + 1), np.arange(half)) % outer)
    return np.concatenate([np.cos(angle), -np.sin(angle)], axis=0).astype(np.float32)


def inner_tables(outer, inner):
    total = outer * inner
    k1 = np.arange(outer // 2 + 1)[:, None, None]
    k2 = np.arange(inner)[None, :, None]
    n2 = np.arange(inner)[None, None, :]
    angle = 2.0 * np.pi / total * (n2 * (k1 + outer * k2) % total)
    c, s = np.cos(angle), np.sin(angle)
    top = np.concatenate([c, s], axis=2)
    low = np.concatenate([-s, c], axis=2)
    return np.concatenate([top, low], axis=1).astype(np.float32)


def local_convolution(signal, kernel):
    length, width = signal.shape
    inner = 128
    outer = 2 * length // inner
    half = outer // 2
    first = jnp.asarray(outer_table(outer))
    second = jnp.asarray(inner_tables(outer, inner))
    both = jnp.concatenate([signal, kernel], axis=1).astype(jnp.float32)
    both = both.reshape(half, inner, 2 * width)
    spread = jnp.einsum("kn,nmc->kmc", first, both, precision=three_pass)
    spread = jnp.concatenate([spread[: half + 1], spread[half + 1 :]], axis=1)
    spectrum = jnp.einsum("kpq,kqc->kpc", second, spread, precision=three_pass)
    real, imag = spectrum[:, :inner], spectrum[:, inner:]
    xr, hr = real[..., :width], real[..., width:]
    xi, hi = imag[..., :width], imag[..., width:]
    product = jnp.concatenate([xr * hr - xi * hi, xr * hi + xi * hr], axis=1)
    back = jnp.einsum("kpq,kpc->kqc", second, product, precision=three_pass)
    stacked = jnp.concatenate([back[:, :inner], back[:, inner:]], axis=0)
    weight = np.full((half + 1,), 2.0)
    weight[0] = weight[-1] = 1.0
    scale = np.concatenate([weight, weight])[:, None] / (2 * length)
    last = jnp.asarray((outer_table(outer) * scale).astype(np.float32))
    rows = jnp.einsum("kn,kmc->nmc", last, stacked, precision=three_pass)
    return rows.reshape(length, width)


def plain_local(raw_query, raw_key, raw_value, short_filter, long_filter, skip, w_out):
    raw_list = [raw.astype(jnp.float32) for raw in (raw_query, raw_key, raw_value)]
    width = raw_list[0].shape[1]
    tail_rows = jnp.concatenate([raw_list[0][-2:], raw_list[1][-2:], raw_list[2][-2:]], axis=1)
    before = passed_along(tail_rows, "ctx", 1)
    filtered = []
    for branch in range(3):
        padded = jnp.concatenate(
            [before[:, branch * width : (branch + 1) * width], raw_list[branch]], axis=0
        )
        filtered.append(
            short_filter[branch, 0] * padded[2:]
            + short_filter[branch, 1] * padded[1:-1]
            + short_filter[branch, 2] * padded[:-2]
        )
    queries, key_rows, value_rows = filtered
    mixed = key_rows * value_rows
    kernel = lax.all_to_all(
        long_filter.astype(jnp.bfloat16), "ctx", split_axis=1, concat_axis=0, tiled=True
    )
    signal = lax.all_to_all(
        mixed.astype(jnp.bfloat16), "ctx", split_axis=1, concat_axis=0, tiled=True
    )
    convolved = local_convolution(signal, kernel).astype(jnp.bfloat16)
    convolved = lax.all_to_all(convolved, "ctx", split_axis=0, concat_axis=1, tiled=True)
    gated = (queries * (convolved.astype(jnp.float32) + skip * mixed)).astype(jnp.bfloat16)
    count = lax.axis_size("chan")
    me = lax.axis_index("chan")
    features = w_out.shape[1] // count

    def share(owner):
        columns = lax.dynamic_slice_in_dim(w_out, owner * features, features, axis=1)
        return jnp.dot(gated, columns, preferred_element_type=jnp.float32)

    arrived = []
    for step in range(1, count):
        pairs = [(source, (source + step) % count) for source in range(count)]
        arrived.append(lax.ppermute(share((me + step) % count).astype(jnp.bfloat16), "chan", pairs))
    summed = share(me)
    for part in arrived:
        summed = summed + part.astype(jnp.float32)
    return summed.astype(jnp.bfloat16)


MESH = pl.DeviceIdType.MESH
LANES = 128
INNER = 128
TILE = 512


def added(a, b):
    if a is None:
        return b
    return a if b is None else a + b


def taken(a, b):
    if b is None:
        return a
    return -b if a is None else a - b


def times(a, c):
    if a is None or abs(c) < 1e-12:
        return None
    if abs(c - 1.0) < 1e-12:
        return a
    return -a if abs(c + 1.0) < 1e-12 else a * np.float32(c)


def turned(pair, angle):
    c, s = math.cos(angle), math.sin(angle)
    re, im = pair
    if re is not None and im is not None and abs(abs(c) - abs(s)) < 1e-12:
        c0 = abs(c)
        sc, ss = (1 if c > 0 else -1), (1 if s > 0 else -1)
        plus, minus = (re + im) * np.float32(c0), (re - im) * np.float32(c0)
        real = minus if sc == ss else plus
        imag = plus if sc == ss else minus
        return (real if sc > 0 else -real), (imag if ss > 0 else -imag)
    return taken(times(re, c), times(im, s)), added(times(re, s), times(im, c))


def forward_real(leaf, start, step, size):
    if size == 2:
        value = leaf(start)
        return [(value, None), (value, None)]
    even = forward_real(leaf, start, 2 * step, size // 2)
    odd = forward_real(leaf, start + step, 2 * step, size // 2)
    half, quarter = size // 2, size // 4
    result = [None] * (half + 1)
    for k in range(quarter + 1):
        re, im = turned(odd[k], -2.0 * math.pi * k / size)
        if k < quarter or quarter == 0:
            far = (taken(even[k][0], re), times(taken(even[k][1], im), -1.0))
            result[half - k] = far
        result[k] = (added(even[k][0], re), added(even[k][1], im))
    return result


def inverse_real(spectrum, size):
    if size == 2:
        return [added(spectrum[0][0], spectrum[1][0])]
    half, quarter = size // 2, size // 4
    even, odd = [], []
    for k in range(quarter + 1):
        near, far = spectrum[k], spectrum[half - k]
        if k == quarter:
            even.append((near[0] + near[0], None))
            odd.append((times(near[1] + near[1], -1.0), None))
            continue
        even.append((added(near[0], far[0]), taken(near[1], far[1])))
        gap = (taken(near[0], far[0]), added(near[1], far[1]))
        odd.append(turned(gap, 2.0 * math.pi * k / size))
    firsts = inverse_real(even, half)
    seconds = inverse_real(odd, half)
    return [value for pair in zip(firsts, seconds) for value in pair]


def exchange(src, dst, send, recv, place):
    return pltpu.make_async_remote_copy(
        src_ref=src, dst_ref=dst, send_sem=send, recv_sem=recv, device_id=place, device_id_type=MESH
    )


def table_product(high, low, values):
    upper = values.astype(jnp.bfloat16)
    lower = (values - upper.astype(jnp.float32)).astype(jnp.bfloat16)
    wide = jnp.concatenate([upper, lower], axis=1)
    first = jnp.dot(high, wide, preferred_element_type=jnp.float32)
    second = jnp.dot(low, upper, preferred_element_type=jnp.float32)
    return first[:, :LANES] + (first[:, LANES:] + second)


def whole_kernel(
    n, q_hbm, k_hbm, v_hbm, taps, h_hbm, skip, w_hbm, fh_hbm, fl_hbm, ih_hbm, il_hbm, out,
    raw, h_all, fh, fl, ih, il, halo, h_send, h_recv, x_send, x_recv, y_recv, queries, direct,
    work, spectrum, gated, weights, p_send, p_recv,
    local_sem, w_sem, halo_s, halo_r, hs, hr, xs, xr, ys, yr, ps, pr,
):
    f32, bf16 = jnp.float32, jnp.bfloat16
    y_send = h_send
    me = lax.axis_index("ctx")
    mine = lax.axis_index("chan")
    other = 1 - mine
    rows = raw.shape[1]
    outer = 4 * n
    half = outer // 2
    entries = half + 1
    group = 3 if entries % 3 == 0 else 1
    features = out.shape[1]
    tiles = features // TILE

    def lanes_of(p):
        return pl.ds(pl.multiple_of(p * LANES, LANES), LANES)

    def weight_copy(i):
        column = lax.rem(other + i // tiles, 2) * features + lax.rem(i, tiles) * TILE
        slot = lax.rem(i, 2)
        return pltpu.make_async_copy(
            w_hbm.at[:, pl.ds(pl.multiple_of(column, TILE), TILE)], weights.at[slot], w_sem.at[slot]
        )

    sources = (h_hbm, k_hbm, v_hbm, q_hbm, fh_hbm, fl_hbm, ih_hbm, il_hbm)
    targets = (h_all, raw.at[1], raw.at[2], raw.at[0], fh, fl, ih, il)
    copies = [
        pltpu.make_async_copy(src, dst, local_sem.at[i]) for i, (src, dst) in enumerate(zip(sources, targets))
    ]
    for copy in copies:
        copy.start()
    weight_copy(0).start()
    weight_copy(1).start()

    barrier = pltpu.get_barrier_semaphore()

    @pl.loop(1, n)
    def _(s):
        pl.semaphore_signal(barrier, inc=1, device_id={"ctx": lax.rem(me + s, n)}, device_id_type=MESH)

    pl.semaphore_signal(barrier, inc=1, device_id={"chan": other}, device_id_type=MESH)
    pl.semaphore_wait(barrier, n)

    after = {"ctx": lax.rem(me + 1, n)}
    tails = [
        exchange(src.at[pl.ds(rows - 16, 16)], halo.at[b], halo_s.at[b], halo_r.at[b], after)
        for b, src in enumerate((q_hbm, k_hbm, v_hbm))
    ]
    for b in (1, 2, 0):
        tails[b].start()

    copies[0].wait()

    @pl.loop(1, n)
    def _(s):
        p = lax.rem(me + s, n)
        h_send[p] = h_all[:, lanes_of(p)].astype(bf16)
        exchange(h_send.at[p], h_recv.at[me], hs.at[p], hr.at[me], {"ctx": p}).start()

    h_recv[me] = h_all[:, lanes_of(me)].astype(bf16)

    place = lax.broadcasted_iota(jnp.int32, (rows, LANES), 0)

    def short(branch, lanes):
        now = raw[branch, :, lanes].astype(f32)
        before = halo[branch, :, lanes].astype(f32)
        before = jnp.where(me > 0, before, 0.0)
        last, former = before[15:16], before[14:15]
        one = jnp.where(place == 0, last, pltpu.roll(now, 1, 0))
        two = jnp.where(place == 0, former, jnp.where(place == 1, last, pltpu.roll(now, 2, 0)))
        tap = [taps[pl.ds(3 * branch + i, 1), lanes] for i in range(3)]
        return tap[0] * now + tap[1] * one + tap[2] * two

    copies[1].wait()
    copies[2].wait()
    tails[1].wait_recv()
    tails[2].wait_recv()

    def mixed_of(p):
        lanes = lanes_of(p)
        mixed = short(1, lanes) * short(2, lanes)
        direct[:, lanes] = skip[:, lanes] * mixed
        return mixed.astype(bf16)

    @pl.loop(1, n)
    def _(s):
        p = lax.rem(me + s, n)
        x_send[p] = mixed_of(p)
        exchange(x_send.at[p], x_recv.at[me], xs.at[p], xr.at[me], {"ctx": p}).start()

    x_recv[me] = mixed_of(me)

    copies[3].wait()
    tails[0].wait_recv()

    @pl.loop(0, n)
    def _(p):
        queries[:, lanes_of(p)] = short(0, lanes_of(p))

    for copy in copies[4:]:
        copy.wait()

    def arrived(refs, p):
        src, dst, send, recv = refs
        return exchange(src.at[p], dst.at[p], send.at[p], recv.at[p], {"ctx": p})

    def wait_all(refs):
        @pl.loop(1, n)
        def _(s):
            arrived(refs, lax.rem(me + s, n)).wait_recv()

    def sent_all(refs):
        @pl.loop(1, n)
        def _(s):
            arrived(refs, lax.rem(me + s, n)).wait_send()

    def outer_forward(received):
        @pl.loop(0, INNER // 16)
        def _(t):
            for part in range(2):
                def leaf(j):
                    begin = pl.multiple_of((j % 2) * INNER + t * 16, 16)
                    return received[j // 2, pl.ds(begin, 16), :].astype(f32)[part * 8 : part * 8 + 8]

                begin = pl.multiple_of(t * 16 + part * 8, 8)
                for k, (re, im) in enumerate(forward_real(leaf, 0, 1, outer)):
                    work[k, pl.ds(begin, 8), :] = re
                    work[k, pl.ds(INNER + begin, 8), :] = jnp.zeros((8, LANES), f32) if im is None else im

    wait_all((h_send, h_recv, hs, hr))
    outer_forward(h_recv)

    @pl.loop(0, entries // group)
    def _(g):
        for j in range(group):
            k = g * group + j
            spectrum[k] = table_product(fh[k], fl[k], work[k])

    wait_all((x_send, x_recv, xs, xr))
    outer_forward(x_recv)

    @pl.loop(0, entries // group)
    def _(g):
        for j in range(group):
            k = g * group + j
            x = table_product(fh[k], fl[k], work[k])
            h = spectrum[k]
            xre, xim, hre, him = x[:INNER], x[INNER:], h[:INNER], h[INNER:]
            product = jnp.concatenate([xre * hre - xim * him, xre * him + xim * hre], axis=0)
            work[k] = table_product(ih[k], il[k], product)

    @pl.loop(0, INNER // 8)
    def _(t):
        begin = pl.multiple_of(t * 8, 8)
        near, far = pl.ds(begin, 8), pl.ds(INNER + begin, 8)
        bins = [(work[k, near, :], work[k, far, :] if 0 < k < half else None) for k in range(entries)]
        for j, value in enumerate(inverse_real(bins, outer)):
            work[j, near, :] = value

    sent_all((h_send, h_recv, hs, hr))
    scale = np.float32(1.0 / (outer * INNER))

    def rows_for(ref, index, p):
        for j in range(2):
            ref[index, pl.ds(j * INNER, INNER), :] = (work[2 * p + j, pl.ds(0, INNER), :] * scale).astype(bf16)

    @pl.loop(1, n)
    def _(s):
        p = lax.rem(me + s, n)
        rows_for(y_send, p, p)
        exchange(y_send.at[p], y_recv.at[me], ys.at[p], yr.at[me], {"ctx": p}).start()

    rows_for(y_recv, me, me)

    def gate(p):
        lanes = lanes_of(p)
        gated[:, lanes] = (queries[:, lanes] * (y_recv[p].astype(f32) + direct[:, lanes])).astype(bf16)

    gate(me)

    @pl.loop(1, n)
    def _(s):
        p = lax.rem(me - s + n, n)
        arrived((y_send, y_recv, ys, yr), p).wait_recv()
        gate(p)

    def partial_copy(i):
        return exchange(p_send.at[i], p_recv.at[i], ps.at[i], pr.at[i], {"chan": other})

    def product_of(i):
        weight_copy(i).wait()
        return jnp.dot(gated[...], weights[lax.rem(i, 2)], preferred_element_type=f32)

    @pl.loop(0, tiles)
    def _(i):
        p_send[i] = product_of(i).astype(bf16)
        partial_copy(i).start()
        weight_copy(i + 2).start()

    @pl.loop(0, tiles)
    def _(i):
        own = product_of(i + tiles)

        @pl.when(i + 2 < tiles)
        def _():
            weight_copy(i + tiles + 2).start()

        partial_copy(i).wait_recv()
        out[:, pl.ds(pl.multiple_of(i * TILE, TILE), TILE)] = (own + p_recv[i].astype(f32)).astype(bf16)

    sent_all((x_send, x_recv, xs, xr))
    sent_all((y_send, y_recv, ys, yr))
    for tail in tails:
        tail.wait_send()

    @pl.loop(0, tiles)
    def _(i):
        partial_copy(i).wait_send()


def fused_local(raw_query, raw_key, raw_value, short_filter, long_filter, skip, w_out):
    n = lax.axis_size("ctx")
    rows, width = raw_query.shape
    features = w_out.shape[1] // 2
    outer = 4 * n
    tiles = features // TILE
    entries = outer // 2 + 1
    table = inner_tables(outer, INNER)
    bf16, f32 = jnp.bfloat16, jnp.float32

    def parts_of(values):
        high = values.astype(bf16)
        low = (values - high.astype(np.float32)).astype(bf16)
        return jnp.asarray(high), jnp.asarray(low)

    fh, fl = parts_of(table)
    ih, il = parts_of(np.ascontiguousarray(table.transpose(0, 2, 1)))
    anywhere = pl.BlockSpec(memory_space=pl.ANY)
    inside = pl.BlockSpec(memory_space=pltpu.VMEM)
    tables = pltpu.VMEM((entries, 2 * INNER, 2 * INNER), bf16)
    blocks = pltpu.VMEM((n, rows, LANES), bf16)
    bins = pltpu.VMEM((entries, 2 * INNER, LANES), f32)
    dma = pltpu.SemaphoreType.DMA
    return pl.pallas_call(
        functools.partial(whole_kernel, n),
        out_shape=jax.ShapeDtypeStruct((rows, features), bf16),
        in_specs=[anywhere] * 3 + [inside, anywhere, inside] + [anywhere] * 5,
        out_specs=inside,
        scratch_shapes=[
            pltpu.VMEM((3, rows, width), bf16),
            pltpu.VMEM((rows, width), f32),
            tables, tables, tables, tables,
            pltpu.VMEM((3, 16, width), bf16),
            blocks, blocks, blocks, blocks, blocks,
            pltpu.VMEM((rows, width), f32),
            pltpu.VMEM((rows, width), f32),
            bins, bins,
            pltpu.VMEM((rows, width), bf16),
            pltpu.VMEM((2, width, TILE), bf16),
            pltpu.VMEM((tiles, rows, TILE), bf16),
            pltpu.VMEM((tiles, rows, TILE), bf16),
            dma((8,)), dma((2,)), dma((3,)), dma((3,)),
            dma((n,)), dma((n,)), dma((n,)), dma((n,)), dma((n,)), dma((n,)),
            dma((tiles,)), dma((tiles,)),
        ],
        compiler_params=pltpu.CompilerParams(
            collective_id=0, has_side_effects=True, vmem_limit_bytes=60 * 1024 * 1024
        ),
    )(
        raw_query, raw_key, raw_value, short_filter.reshape(9, width), long_filter,
        skip.reshape(1, width), w_out, fh, fl, ih, il,
    )


def local(*arrays):
    rows, width = arrays[0].shape
    n = lax.axis_size("ctx")
    fits = lax.axis_size("chan") == 2 and rows == 2 * INNER and width == n * LANES
    fits = fits and n & (n - 1) == 0 and n <= 16 and arrays[6].shape[1] % (4 * TILE) == 0
    return fused_local(*arrays) if fits else plain_local(*arrays)


def solution(mesh):
    in_specs = (
        P("ctx", "chan"),
        P("ctx", "chan"),
        P("ctx", "chan"),
        P(None, None, "chan"),
        P("ctx", "chan"),
        P("chan"),
        P("chan", None),
    )
    out_specs = P("ctx", "chan")
    return jax.shard_map(local, mesh=mesh, in_specs=in_specs, out_specs=out_specs, check_vma=False)
```

```python
import functools
import math

import jax
import jax.numpy as jnp
import numpy as np
from jax import lax
from jax.experimental import pallas as pl
from jax.experimental.pallas import tpu as pltpu
from jax.sharding import PartitionSpec as P

three_pass = lax.Precision.HIGH


def passed_along(value, axis, steps):
    count = lax.axis_size(axis)
    first, last = (max(0, -steps), min(count, count - steps))
    return lax.ppermute(value, axis, [(source, source + steps) for source in range(first, last)])


def outer_table(outer):
    half = outer // 2
    angle = 2.0 * np.pi / outer * (np.outer(np.arange(half + 1), np.arange(half)) % outer)
    return np.concatenate([np.cos(angle), -np.sin(angle)], axis=0).astype(np.float32)


def inner_tables(outer, inner):
    total = outer * inner
    k1 = np.arange(outer // 2 + 1)[:, None, None]
    k2 = np.arange(inner)[None, :, None]
    n2 = np.arange(inner)[None, None, :]
    angle = 2.0 * np.pi / total * (n2 * (k1 + outer * k2) % total)
    c, s = np.cos(angle), np.sin(angle)
    top = np.concatenate([c, s], axis=2)
    low = np.concatenate([-s, c], axis=2)
    return np.concatenate([top, low], axis=1).astype(np.float32)


def local_convolution(signal, kernel):
    length, width = signal.shape
    inner = 128
    outer = 2 * length // inner
    half = outer // 2
    first = jnp.asarray(outer_table(outer))
    second = jnp.asarray(inner_tables(outer, inner))
    both = jnp.concatenate([signal, kernel], axis=1).astype(jnp.float32)
    both = both.reshape(half, inner, 2 * width)
    spread = jnp.einsum("kn,nmc->kmc", first, both, precision=three_pass)
    spread = jnp.concatenate([spread[: half + 1], spread[half + 1 :]], axis=1)
    spectrum = jnp.einsum("kpq,kqc->kpc", second, spread, precision=three_pass)
    real, imag = spectrum[:, :inner], spectrum[:, inner:]
    xr, hr = real[..., :width], real[..., width:]
    xi, hi = imag[..., :width], imag[..., width:]
    product = jnp.concatenate([xr * hr - xi * hi, xr * hi + xi * hr], axis=1)
    back = jnp.einsum("kpq,kpc->kqc", second, product, precision=three_pass)
    stacked = jnp.concatenate([back[:, :inner], back[:, inner:]], axis=0)
    weight = np.full((half + 1,), 2.0)
    weight[0] = weight[-1] = 1.0
    scale = np.concatenate([weight, weight])[:, None] / (2 * length)
    last = jnp.asarray((outer_table(outer) * scale).astype(np.float32))
    rows = jnp.einsum("kn,kmc->nmc", last, stacked, precision=three_pass)
    return rows.reshape(length, width)


def plain_local(raw_query, raw_key, raw_value, short_filter, long_filter, skip, w_out):
    raw_list = [raw.astype(jnp.float32) for raw in (raw_query, raw_key, raw_value)]
    width = raw_list[0].shape[1]
    tail_rows = jnp.concatenate([raw_list[0][-2:], raw_list[1][-2:], raw_list[2][-2:]], axis=1)
    before = passed_along(tail_rows, "ctx", 1)
    filtered = []
    for branch in range(3):
        padded = jnp.concatenate(
            [before[:, branch * width : (branch + 1) * width], raw_list[branch]], axis=0
        )
        filtered.append(
            short_filter[branch, 0] * padded[2:]
            + short_filter[branch, 1] * padded[1:-1]
            + short_filter[branch, 2] * padded[:-2]
        )
    queries, key_rows, value_rows = filtered
    mixed = key_rows * value_rows
    kernel = lax.all_to_all(
        long_filter.astype(jnp.bfloat16), "ctx", split_axis=1, concat_axis=0, tiled=True
    )
    signal = lax.all_to_all(
        mixed.astype(jnp.bfloat16), "ctx", split_axis=1, concat_axis=0, tiled=True
    )
    convolved = local_convolution(signal, kernel).astype(jnp.bfloat16)
    convolved = lax.all_to_all(convolved, "ctx", split_axis=0, concat_axis=1, tiled=True)
    gated = (queries * (convolved.astype(jnp.float32) + skip * mixed)).astype(jnp.bfloat16)
    count = lax.axis_size("chan")
    me = lax.axis_index("chan")
    features = w_out.shape[1] // count

    def share(owner):
        columns = lax.dynamic_slice_in_dim(w_out, owner * features, features, axis=1)
        return jnp.dot(gated, columns, preferred_element_type=jnp.float32)

    arrived = []
    for step in range(1, count):
        pairs = [(source, (source + step) % count) for source in range(count)]
        arrived.append(lax.ppermute(share((me + step) % count).astype(jnp.bfloat16), "chan", pairs))
    summed = share(me)
    for part in arrived:
        summed = summed + part.astype(jnp.float32)
    return summed.astype(jnp.bfloat16)


MESH = pl.DeviceIdType.MESH
LANES = 128
INNER = 128
TILE = 512
CHUNKS = 2


def added(a, b):
    if a is None:
        return b
    return a if b is None else a + b


def taken(a, b):
    if b is None:
        return a
    return -b if a is None else a - b


def times(a, c):
    if a is None or abs(c) < 1e-12:
        return None
    if abs(c - 1.0) < 1e-12:
        return a
    return -a if abs(c + 1.0) < 1e-12 else a * np.float32(c)


def turned(pair, angle):
    c, s = math.cos(angle), math.sin(angle)
    re, im = pair
    if re is not None and im is not None and abs(abs(c) - abs(s)) < 1e-12:
        c0 = abs(c)
        sc, ss = (1 if c > 0 else -1), (1 if s > 0 else -1)
        plus, minus = (re + im) * np.float32(c0), (re - im) * np.float32(c0)
        real = minus if sc == ss else plus
        imag = plus if sc == ss else minus
        return (real if sc > 0 else -real), (imag if ss > 0 else -imag)
    return taken(times(re, c), times(im, s)), added(times(re, s), times(im, c))


def forward_real(leaf, start, step, size):
    if size == 2:
        value = leaf(start)
        return [(value, None), (value, None)]
    even = forward_real(leaf, start, 2 * step, size // 2)
    odd = forward_real(leaf, start + step, 2 * step, size // 2)
    half, quarter = size // 2, size // 4
    result = [None] * (half + 1)
    for k in range(quarter + 1):
        re, im = turned(odd[k], -2.0 * math.pi * k / size)
        if k < quarter or quarter == 0:
            far = (taken(even[k][0], re), times(taken(even[k][1], im), -1.0))
            result[half - k] = far
        result[k] = (added(even[k][0], re), added(even[k][1], im))
    return result


def inverse_real(spectrum, size):
    if size == 2:
        return [added(spectrum[0][0], spectrum[1][0])]
    half, quarter = size // 2, size // 4
    even, odd = [], []
    for k in range(quarter + 1):
        near, far = spectrum[k], spectrum[half - k]
        if k == quarter:
            even.append((near[0] + near[0], None))
            odd.append((times(near[1] + near[1], -1.0), None))
            continue
        even.append((added(near[0], far[0]), taken(near[1], far[1])))
        gap = (taken(near[0], far[0]), added(near[1], far[1]))
        odd.append(turned(gap, 2.0 * math.pi * k / size))
    firsts = inverse_real(even, half)
    seconds = inverse_real(odd, half)
    return [value for pair in zip(firsts, seconds) for value in pair]


def exchange(src, dst, send, recv, place):
    return pltpu.make_async_remote_copy(
        src_ref=src, dst_ref=dst, send_sem=send, recv_sem=recv, device_id=place, device_id_type=MESH
    )


def table_product(high, low, values):
    upper = values.astype(jnp.bfloat16)
    lower = (values - upper.astype(jnp.float32)).astype(jnp.bfloat16)
    wide = jnp.concatenate([upper, lower], axis=1)
    first = jnp.dot(high, wide, preferred_element_type=jnp.float32)
    second = jnp.dot(low, upper, preferred_element_type=jnp.float32)
    return first[:, :LANES] + (first[:, LANES:] + second)


def whole_kernel(
    n, q_hbm, k_hbm, v_hbm, taps, h_hbm, skip, w_hbm, fh_hbm, fl_hbm, ih_hbm, il_hbm, out,
    raw, h_all, fh, fl, ih, il, halo, h_send, h_recv, x_send, x_recv, y_recv, queries, direct,
    work, spectrum, gated, weights, p_send, p_recv,
    local_sem, w_sem, halo_s, halo_r, hs, hr, xs, xr, ys, yr, ps, pr,
):
    f32, bf16 = jnp.float32, jnp.bfloat16
    y_send = h_send
    me = lax.axis_index("ctx")
    mine = lax.axis_index("chan")
    other = 1 - mine
    rows = raw.shape[1]
    outer = 4 * n
    half = outer // 2
    entries = half + 1
    group = next(size for size in (11, 3, 1) if entries % size == 0)
    features = out.shape[1]
    tiles = features // TILE

    def lanes_of(p):
        return pl.ds(pl.multiple_of(p * LANES, LANES), LANES)

    def weight_copy(i):
        column = lax.rem(other + i // (CHUNKS * tiles), 2) * features + lax.rem(i, tiles) * TILE
        slot = lax.rem(i, 2)
        return pltpu.make_async_copy(
            w_hbm.at[:, pl.ds(pl.multiple_of(column, TILE), TILE)], weights.at[slot], w_sem.at[slot]
        )

    side, spot, span = me // (n // 2), lax.rem(me, n // 2), n // 2

    def each_peer(visit):
        @pl.loop(0, span)
        def _(j):
            step = lax.rem(spot + j, span)
            visit((1 - side) * span + step)

            @pl.when(j > 0)
            def _():
                visit(side * span + step)

    sources = (h_hbm, k_hbm, v_hbm, q_hbm, fh_hbm, fl_hbm, ih_hbm, il_hbm)
    targets = (h_all, raw.at[1], raw.at[2], raw.at[0], fh, fl, ih, il)
    copies = [
        pltpu.make_async_copy(src, dst, local_sem.at[i]) for i, (src, dst) in enumerate(zip(sources, targets))
    ]
    for copy in copies:
        copy.start()
    weight_copy(0).start()
    weight_copy(1).start()

    barrier = pltpu.get_barrier_semaphore()

    @pl.loop(1, n)
    def _(s):
        pl.semaphore_signal(barrier, inc=1, device_id={"ctx": lax.rem(me + s, n)}, device_id_type=MESH)

    pl.semaphore_signal(barrier, inc=1, device_id={"chan": other}, device_id_type=MESH)
    pl.semaphore_wait(barrier, n)

    after = {"ctx": lax.rem(me + 1, n)}
    tails = [
        exchange(src.at[pl.ds(rows - 16, 16)], halo.at[b], halo_s.at[b], halo_r.at[b], after)
        for b, src in enumerate((q_hbm, k_hbm, v_hbm))
    ]
    for b in (1, 2, 0):
        tails[b].start()

    copies[0].wait()

    @each_peer
    def _(p):
        h_send[p] = h_all[:, lanes_of(p)].astype(bf16)
        exchange(h_send.at[p], h_recv.at[me], hs.at[p], hr.at[me], {"ctx": p}).start()

    h_recv[me] = h_all[:, lanes_of(me)].astype(bf16)

    place = lax.broadcasted_iota(jnp.int32, (rows, LANES), 0)

    def short(branch, lanes):
        now = raw[branch, :, lanes].astype(f32)
        before = halo[branch, :, lanes].astype(f32)
        before = jnp.where(me > 0, before, 0.0)
        last, former = before[15:16], before[14:15]
        one = jnp.where(place == 0, last, pltpu.roll(now, 1, 0))
        two = jnp.where(place == 0, former, jnp.where(place == 1, last, pltpu.roll(now, 2, 0)))
        tap = [taps[branch, pl.ds(i, 1), lanes] for i in range(3)]
        return tap[0] * now + tap[1] * one + tap[2] * two

    copies[1].wait()
    copies[2].wait()
    tails[1].wait_recv()
    tails[2].wait_recv()

    def mixed_of(p):
        lanes = lanes_of(p)
        mixed = short(1, lanes) * short(2, lanes)
        direct[:, lanes] = skip[:, lanes] * mixed
        return mixed.astype(bf16)

    @each_peer
    def _(p):
        x_send[p] = mixed_of(p)
        exchange(x_send.at[p], x_recv.at[me], xs.at[p], xr.at[me], {"ctx": p}).start()

    x_recv[me] = mixed_of(me)

    copies[3].wait()
    tails[0].wait_recv()

    @pl.loop(0, n)
    def _(p):
        queries[:, lanes_of(p)] = short(0, lanes_of(p))

    for copy in copies[4:]:
        copy.wait()

    def arrived(refs, p):
        src, dst, send, recv = refs
        return exchange(src.at[p], dst.at[p], send.at[p], recv.at[p], {"ctx": p})

    def wait_all(refs):
        @pl.loop(1, n)
        def _(s):
            arrived(refs, lax.rem(me + s, n)).wait_recv()

    def sent_all(refs):
        @pl.loop(1, n)
        def _(s):
            arrived(refs, lax.rem(me + s, n)).wait_send()

    def outer_forward(received):
        @pl.loop(0, INNER // 16)
        def _(t):
            for part in range(2):
                def leaf(j):
                    begin = pl.multiple_of((j % 2) * INNER + t * 16, 16)
                    return received[j // 2, pl.ds(begin, 16), :].astype(f32)[part * 8 : part * 8 + 8]

                begin = pl.multiple_of(t * 16 + part * 8, 8)
                for k, (re, im) in enumerate(forward_real(leaf, 0, 1, outer)):
                    work[k, pl.ds(begin, 8), :] = re
                    work[k, pl.ds(INNER + begin, 8), :] = jnp.zeros((8, LANES), f32) if im is None else im

    wait_all((h_send, h_recv, hs, hr))
    outer_forward(h_recv)

    @pl.loop(0, entries // group)
    def _(g):
        ks = [g * group + j for j in range(group)]
        made = [table_product(fh[k], fl[k], work[k]) for k in ks]
        for k, value in zip(ks, made):
            spectrum[k] = value

    wait_all((x_send, x_recv, xs, xr))
    outer_forward(x_recv)

    @pl.loop(0, entries // group)
    def _(g):
        ks = [g * group + j for j in range(group)]
        signals = [table_product(fh[k], fl[k], work[k]) for k in ks]
        products = []
        for k, x in zip(ks, signals):
            h = spectrum[k]
            xre, xim, hre, him = x[:INNER], x[INNER:], h[:INNER], h[INNER:]
            products.append(jnp.concatenate([xre * hre - xim * him, xre * him + xim * hre], axis=0))
        made = [table_product(ih[k], il[k], product) for k, product in zip(ks, products)]
        for k, value in zip(ks, made):
            work[k] = value

    sent_all((h_send, h_recv, hs, hr))
    scale = np.float32(1.0 / (outer * INNER))
    piece = INNER // CHUNKS
    height = rows // CHUNKS

    def rows_for(ref, index, p, q):
        for j in range(2):
            value = work[2 * p + j, pl.ds(q * piece, piece), :] * scale
            ref[index, pl.ds(q * height + j * piece, piece), :] = value.astype(bf16)

    def returned(p, q, source):
        part = pl.ds(q * height, height)
        return exchange(
            y_send.at[p, part], y_recv.at[source, part], ys.at[q * n + p], yr.at[q * n + source], {"ctx": p}
        )

    for q in range(CHUNKS):
        @pl.loop(q * (piece // 8), (q + 1) * (piece // 8))
        def _(t):
            begin = pl.multiple_of(t * 8, 8)
            near, far = pl.ds(begin, 8), pl.ds(INNER + begin, 8)
            bins = [(work[k, near, :], work[k, far, :] if 0 < k < half else None) for k in range(entries)]
            for j, value in enumerate(inverse_real(bins, outer)):
                work[j, near, :] = value

        @each_peer
        def _(p):
            rows_for(y_send, p, p, q)
            returned(p, q, me).start()

        rows_for(y_recv, me, me, q)

    def gate(p, q):
        lanes = lanes_of(p)
        for j in range(2):
            there, here = pl.ds(j * INNER + q * piece, piece), pl.ds(q * height + j * piece, piece)
            sum_of = y_recv[p, here, :].astype(f32) + direct[there, lanes]
            gated[here, lanes] = (queries[there, lanes] * sum_of).astype(bf16)

    def partial_copy(i):
        return exchange(p_send.at[i], p_recv.at[i], ps.at[i], pr.at[i], {"chan": other})

    for q in range(CHUNKS):
        gate(me, q)

        @each_peer
        def _(p):
            returned(p, q, p).wait_recv()
            gate(p, q)

        @pl.loop(q * tiles, (q + 1) * tiles)
        def _(i):
            weight_copy(i).wait()
            left = gated[pl.ds(q * height, height), :]
            part = jnp.dot(left, weights[lax.rem(i, 2)], preferred_element_type=f32)
            p_send[i] = part.astype(bf16)
            partial_copy(i).start()
            weight_copy(i + 2).start()

    @pl.loop(0, tiles)
    def _(i):
        number = i + CHUNKS * tiles
        weight_copy(number).wait()
        own = jnp.dot(gated[...], weights[lax.rem(number, 2)], preferred_element_type=f32)

        @pl.when(i + 2 < tiles)
        def _():
            weight_copy(number + 2).start()

        columns = pl.ds(pl.multiple_of(i * TILE, TILE), TILE)
        for q in range(CHUNKS):
            partial_copy(q * tiles + i).wait_recv()
            for j in range(2):
                begin = q * height + j * piece
                came = p_recv[q * tiles + i, pl.ds(j * piece, piece), :].astype(f32)
                out[pl.ds(j * INNER + q * piece, piece), columns] = (own[begin : begin + piece] + came).astype(bf16)

    sent_all((x_send, x_recv, xs, xr))
    for q in range(CHUNKS):
        @each_peer
        def _(p):
            returned(p, q, me).wait_send()

    for tail in tails:
        tail.wait_send()

    @pl.loop(0, CHUNKS * tiles)
    def _(i):
        partial_copy(i).wait_send()


def fused_local(raw_query, raw_key, raw_value, short_filter, long_filter, skip, w_out):
    n = lax.axis_size("ctx")
    rows, width = raw_query.shape
    features = w_out.shape[1] // 2
    outer = 4 * n
    tiles = features // TILE
    entries = outer // 2 + 1
    table = inner_tables(outer, INNER)
    bf16, f32 = jnp.bfloat16, jnp.float32

    def parts_of(values):
        high = values.astype(bf16)
        low = (values - high.astype(np.float32)).astype(bf16)
        return jnp.asarray(high), jnp.asarray(low)

    fh, fl = parts_of(table)
    ih, il = parts_of(np.ascontiguousarray(table.transpose(0, 2, 1)))
    anywhere = pl.BlockSpec(memory_space=pl.ANY)
    inside = pl.BlockSpec(memory_space=pltpu.VMEM)
    tables = pltpu.VMEM((entries, 2 * INNER, 2 * INNER), bf16)
    blocks = pltpu.VMEM((n, rows, LANES), bf16)
    bins = pltpu.VMEM((entries, 2 * INNER, LANES), f32)
    dma = pltpu.SemaphoreType.DMA
    return pl.pallas_call(
        functools.partial(whole_kernel, n),
        out_shape=jax.ShapeDtypeStruct((rows, features), bf16),
        in_specs=[anywhere] * 3 + [inside, anywhere, inside] + [anywhere] * 5,
        out_specs=inside,
        scratch_shapes=[
            pltpu.VMEM((3, rows, width), bf16),
            pltpu.VMEM((rows, width), f32),
            tables, tables, tables, tables,
            pltpu.VMEM((3, 16, width), bf16),
            blocks, blocks, blocks, blocks, blocks,
            pltpu.VMEM((rows, width), f32),
            pltpu.VMEM((rows, width), f32),
            bins, bins,
            pltpu.VMEM((rows, width), bf16),
            pltpu.VMEM((2, width, TILE), bf16),
            pltpu.VMEM((CHUNKS * tiles, rows // CHUNKS, TILE), bf16),
            pltpu.VMEM((CHUNKS * tiles, rows // CHUNKS, TILE), bf16),
            dma((8,)), dma((2,)), dma((3,)), dma((3,)),
            dma((n,)), dma((n,)), dma((n,)), dma((n,)), dma((CHUNKS * n,)), dma((CHUNKS * n,)),
            dma((CHUNKS * tiles,)), dma((CHUNKS * tiles,)),
        ],
        compiler_params=pltpu.CompilerParams(
            collective_id=0, has_side_effects=True, vmem_limit_bytes=60 * 1024 * 1024
        ),
    )(
        raw_query, raw_key, raw_value, short_filter, long_filter,
        skip.reshape(1, width), w_out, fh, fl, ih, il,
    )


def local(*arrays):
    rows, width = arrays[0].shape
    n = lax.axis_size("ctx")
    fits = lax.axis_size("chan") == 2 and rows == 2 * INNER and width == n * LANES
    fits = fits and n & (n - 1) == 0 and n <= 16 and arrays[6].shape[1] % (4 * TILE) == 0
    return fused_local(*arrays) if fits else plain_local(*arrays)


def solution(mesh):
    in_specs = (
        P("ctx", "chan"),
        P("ctx", "chan"),
        P("ctx", "chan"),
        P(None, None, "chan"),
        P("ctx", "chan"),
        P("chan"),
        P("chan", None),
    )
    out_specs = P("ctx", "chan")
    return jax.shard_map(local, mesh=mesh, in_specs=in_specs, out_specs=out_specs, check_vma=False)
```

```python
import functools
import math

import jax
import jax.numpy as jnp
import numpy as np
from jax import lax
from jax.experimental import pallas as pl
from jax.experimental.pallas import tpu as pltpu
from jax.sharding import PartitionSpec as P

three_pass = lax.Precision.HIGH


def passed_along(value, axis, steps):
    count = lax.axis_size(axis)
    first, last = (max(0, -steps), min(count, count - steps))
    return lax.ppermute(value, axis, [(source, source + steps) for source in range(first, last)])


def outer_table(outer):
    half = outer // 2
    angle = 2.0 * np.pi / outer * (np.outer(np.arange(half + 1), np.arange(half)) % outer)
    return np.concatenate([np.cos(angle), -np.sin(angle)], axis=0).astype(np.float32)


def inner_tables(outer, inner):
    total = outer * inner
    k1 = np.arange(outer // 2 + 1)[:, None, None]
    k2 = np.arange(inner)[None, :, None]
    n2 = np.arange(inner)[None, None, :]
    angle = 2.0 * np.pi / total * (n2 * (k1 + outer * k2) % total)
    c, s = np.cos(angle), np.sin(angle)
    top = np.concatenate([c, s], axis=2)
    low = np.concatenate([-s, c], axis=2)
    return np.concatenate([top, low], axis=1).astype(np.float32)


def local_convolution(signal, kernel):
    length, width = signal.shape
    inner = 128
    outer = 2 * length // inner
    half = outer // 2
    first = jnp.asarray(outer_table(outer))
    second = jnp.asarray(inner_tables(outer, inner))
    both = jnp.concatenate([signal, kernel], axis=1).astype(jnp.float32)
    both = both.reshape(half, inner, 2 * width)
    spread = jnp.einsum("kn,nmc->kmc", first, both, precision=three_pass)
    spread = jnp.concatenate([spread[: half + 1], spread[half + 1 :]], axis=1)
    spectrum = jnp.einsum("kpq,kqc->kpc", second, spread, precision=three_pass)
    real, imag = spectrum[:, :inner], spectrum[:, inner:]
    xr, hr = real[..., :width], real[..., width:]
    xi, hi = imag[..., :width], imag[..., width:]
    product = jnp.concatenate([xr * hr - xi * hi, xr * hi + xi * hr], axis=1)
    back = jnp.einsum("kpq,kpc->kqc", second, product, precision=three_pass)
    stacked = jnp.concatenate([back[:, :inner], back[:, inner:]], axis=0)
    weight = np.full((half + 1,), 2.0)
    weight[0] = weight[-1] = 1.0
    scale = np.concatenate([weight, weight])[:, None] / (2 * length)
    last = jnp.asarray((outer_table(outer) * scale).astype(np.float32))
    rows = jnp.einsum("kn,kmc->nmc", last, stacked, precision=three_pass)
    return rows.reshape(length, width)


def plain_local(raw_query, raw_key, raw_value, short_filter, long_filter, skip, w_out):
    raw_list = [raw.astype(jnp.float32) for raw in (raw_query, raw_key, raw_value)]
    width = raw_list[0].shape[1]
    tail_rows = jnp.concatenate([raw_list[0][-2:], raw_list[1][-2:], raw_list[2][-2:]], axis=1)
    before = passed_along(tail_rows, "ctx", 1)
    filtered = []
    for branch in range(3):
        padded = jnp.concatenate(
            [before[:, branch * width : (branch + 1) * width], raw_list[branch]], axis=0
        )
        filtered.append(
            short_filter[branch, 0] * padded[2:]
            + short_filter[branch, 1] * padded[1:-1]
            + short_filter[branch, 2] * padded[:-2]
        )
    queries, key_rows, value_rows = filtered
    mixed = key_rows * value_rows
    kernel = lax.all_to_all(
        long_filter.astype(jnp.bfloat16), "ctx", split_axis=1, concat_axis=0, tiled=True
    )
    signal = lax.all_to_all(
        mixed.astype(jnp.bfloat16), "ctx", split_axis=1, concat_axis=0, tiled=True
    )
    convolved = local_convolution(signal, kernel).astype(jnp.bfloat16)
    convolved = lax.all_to_all(convolved, "ctx", split_axis=0, concat_axis=1, tiled=True)
    gated = (queries * (convolved.astype(jnp.float32) + skip * mixed)).astype(jnp.bfloat16)
    count = lax.axis_size("chan")
    me = lax.axis_index("chan")
    features = w_out.shape[1] // count

    def share(owner):
        columns = lax.dynamic_slice_in_dim(w_out, owner * features, features, axis=1)
        return jnp.dot(gated, columns, preferred_element_type=jnp.float32)

    arrived = []
    for step in range(1, count):
        pairs = [(source, (source + step) % count) for source in range(count)]
        arrived.append(lax.ppermute(share((me + step) % count).astype(jnp.bfloat16), "chan", pairs))
    summed = share(me)
    for part in arrived:
        summed = summed + part.astype(jnp.float32)
    return summed.astype(jnp.bfloat16)


MESH = pl.DeviceIdType.MESH
LANES = 128
INNER = 128
TILE = 512
CHUNKS = 4


def added(a, b):
    if a is None:
        return b
    return a if b is None else a + b


def taken(a, b):
    if b is None:
        return a
    return -b if a is None else a - b


def times(a, c):
    if a is None or abs(c) < 1e-12:
        return None
    if abs(c - 1.0) < 1e-12:
        return a
    return -a if abs(c + 1.0) < 1e-12 else a * np.float32(c)


def turned(pair, angle):
    c, s = math.cos(angle), math.sin(angle)
    re, im = pair
    if re is not None and im is not None and abs(abs(c) - abs(s)) < 1e-12:
        c0 = abs(c)
        sc, ss = (1 if c > 0 else -1), (1 if s > 0 else -1)
        plus, minus = (re + im) * np.float32(c0), (re - im) * np.float32(c0)
        real = minus if sc == ss else plus
        imag = plus if sc == ss else minus
        return (real if sc > 0 else -real), (imag if ss > 0 else -imag)
    return taken(times(re, c), times(im, s)), added(times(re, s), times(im, c))


def forward_real(leaf, start, step, size):
    if size == 2:
        value = leaf(start)
        return [(value, None), (value, None)]
    even = forward_real(leaf, start, 2 * step, size // 2)
    odd = forward_real(leaf, start + step, 2 * step, size // 2)
    half, quarter = size // 2, size // 4
    result = [None] * (half + 1)
    for k in range(quarter + 1):
        re, im = turned(odd[k], -2.0 * math.pi * k / size)
        if k < quarter or quarter == 0:
            far = (taken(even[k][0], re), times(taken(even[k][1], im), -1.0))
            result[half - k] = far
        result[k] = (added(even[k][0], re), added(even[k][1], im))
    return result


def inverse_real(spectrum, size):
    if size == 2:
        return [added(spectrum[0][0], spectrum[1][0])]
    half, quarter = size // 2, size // 4
    even, odd = [], []
    for k in range(quarter + 1):
        near, far = spectrum[k], spectrum[half - k]
        if k == quarter:
            even.append((near[0] + near[0], None))
            odd.append((times(near[1] + near[1], -1.0), None))
            continue
        even.append((added(near[0], far[0]), taken(near[1], far[1])))
        gap = (taken(near[0], far[0]), added(near[1], far[1]))
        odd.append(turned(gap, 2.0 * math.pi * k / size))
    firsts = inverse_real(even, half)
    seconds = inverse_real(odd, half)
    return [value for pair in zip(firsts, seconds) for value in pair]


def exchange(src, dst, send, recv, place):
    return pltpu.make_async_remote_copy(
        src_ref=src, dst_ref=dst, send_sem=send, recv_sem=recv, device_id=place, device_id_type=MESH
    )


def table_product(high, low, values):
    upper = values.astype(jnp.bfloat16)
    lower = (values - upper.astype(jnp.float32)).astype(jnp.bfloat16)
    wide = jnp.concatenate([upper, lower], axis=1)
    first = jnp.dot(high, wide, preferred_element_type=jnp.float32)
    second = jnp.dot(low, upper, preferred_element_type=jnp.float32)
    return first[:, :LANES] + (first[:, LANES:] + second)


def whole_kernel(
    n, q_hbm, k_hbm, v_hbm, taps, h_hbm, skip, w_hbm, fh_hbm, fl_hbm, ih_hbm, il_hbm, out,
    raw, h_all, fh, fl, ih, il, halo, h_send, h_recv, x_send, x_recv, y_recv, queries, direct,
    work, spectrum, gated, weights, p_send, p_recv,
    local_sem, w_sem, halo_s, halo_r, hs, hr, xs, xr, ys, yr, ps, pr,
):
    f32, bf16 = jnp.float32, jnp.bfloat16
    y_send = h_send
    me = lax.axis_index("ctx")
    mine = lax.axis_index("chan")
    other = 1 - mine
    rows = raw.shape[1]
    outer = 4 * n
    half = outer // 2
    entries = half + 1
    group = next(size for size in (11, 3, 1) if entries % size == 0)
    features = out.shape[1]
    tiles = features // TILE

    def lanes_of(p):
        return pl.ds(pl.multiple_of(p * LANES, LANES), LANES)

    def weight_copy(i):
        column = lax.rem(other + i // (CHUNKS * tiles), 2) * features + lax.rem(i, tiles) * TILE
        slot = lax.rem(i, 2)
        return pltpu.make_async_copy(
            w_hbm.at[:, pl.ds(pl.multiple_of(column, TILE), TILE)], weights.at[slot], w_sem.at[slot]
        )

    side, spot, span = me // (n // 2), lax.rem(me, n // 2), n // 2

    def each_peer(visit):
        @pl.loop(0, span)
        def _(j):
            step = lax.rem(spot + j, span)
            visit((1 - side) * span + step)

            @pl.when(j > 0)
            def _():
                visit(side * span + step)

    sources = (h_hbm, k_hbm, v_hbm, q_hbm, fh_hbm, fl_hbm, ih_hbm, il_hbm)
    targets = (h_all, raw.at[1], raw.at[2], raw.at[0], fh, fl, ih, il)
    copies = [
        pltpu.make_async_copy(src, dst, local_sem.at[i]) for i, (src, dst) in enumerate(zip(sources, targets))
    ]
    for copy in copies:
        copy.start()
    weight_copy(0).start()
    weight_copy(1).start()

    barrier = pltpu.get_barrier_semaphore()

    @pl.loop(1, n)
    def _(s):
        pl.semaphore_signal(barrier, inc=1, device_id={"ctx": lax.rem(me + s, n)}, device_id_type=MESH)

    pl.semaphore_signal(barrier, inc=1, device_id={"chan": other}, device_id_type=MESH)
    pl.semaphore_wait(barrier, n)

    after = {"ctx": lax.rem(me + 1, n)}
    tails = [
        exchange(src.at[pl.ds(rows - 16, 16)], halo.at[b], halo_s.at[b], halo_r.at[b], after)
        for b, src in enumerate((q_hbm, k_hbm, v_hbm))
    ]
    for b in (1, 2, 0):
        tails[b].start()

    copies[0].wait()

    @each_peer
    def _(p):
        h_send[p] = h_all[:, lanes_of(p)].astype(bf16)
        exchange(h_send.at[p], h_recv.at[me], hs.at[p], hr.at[me], {"ctx": p}).start()

    h_recv[me] = h_all[:, lanes_of(me)].astype(bf16)

    place = lax.broadcasted_iota(jnp.int32, (rows, LANES), 0)

    def short(branch, lanes):
        now = raw[branch, :, lanes].astype(f32)
        before = halo[branch, :, lanes].astype(f32)
        before = jnp.where(me > 0, before, 0.0)
        last, former = before[15:16], before[14:15]
        one = jnp.where(place == 0, last, pltpu.roll(now, 1, 0))
        two = jnp.where(place == 0, former, jnp.where(place == 1, last, pltpu.roll(now, 2, 0)))
        tap = [taps[branch, pl.ds(i, 1), lanes] for i in range(3)]
        return tap[0] * now + tap[1] * one + tap[2] * two

    copies[1].wait()
    copies[2].wait()
    tails[1].wait_recv()
    tails[2].wait_recv()

    def mixed_of(p):
        lanes = lanes_of(p)
        mixed = short(1, lanes) * short(2, lanes)
        direct[:, lanes] = skip[:, lanes] * mixed
        return mixed.astype(bf16)

    @each_peer
    def _(p):
        x_send[p] = mixed_of(p)
        exchange(x_send.at[p], x_recv.at[me], xs.at[p], xr.at[me], {"ctx": p}).start()

    x_recv[me] = mixed_of(me)

    copies[3].wait()
    tails[0].wait_recv()

    @pl.loop(0, n)
    def _(p):
        queries[:, lanes_of(p)] = short(0, lanes_of(p))

    for copy in copies[4:]:
        copy.wait()

    def arrived(refs, p):
        src, dst, send, recv = refs
        return exchange(src.at[p], dst.at[p], send.at[p], recv.at[p], {"ctx": p})

    def wait_all(refs):
        @pl.loop(1, n)
        def _(s):
            arrived(refs, lax.rem(me + s, n)).wait_recv()

    def sent_all(refs):
        @pl.loop(1, n)
        def _(s):
            arrived(refs, lax.rem(me + s, n)).wait_send()

    def outer_forward(received):
        @pl.loop(0, INNER // 16)
        def _(t):
            for part in range(2):
                def leaf(j):
                    begin = pl.multiple_of((j % 2) * INNER + t * 16, 16)
                    return received[j // 2, pl.ds(begin, 16), :].astype(f32)[part * 8 : part * 8 + 8]

                begin = pl.multiple_of(t * 16 + part * 8, 8)
                for k, (re, im) in enumerate(forward_real(leaf, 0, 1, outer)):
                    work[k, pl.ds(begin, 8), :] = re
                    work[k, pl.ds(INNER + begin, 8), :] = jnp.zeros((8, LANES), f32) if im is None else im

    wait_all((h_send, h_recv, hs, hr))
    outer_forward(h_recv)

    @pl.loop(0, entries // group)
    def _(g):
        ks = [g * group + j for j in range(group)]
        made = [table_product(fh[k], fl[k], work[k]) for k in ks]
        for k, value in zip(ks, made):
            spectrum[k] = value

    wait_all((x_send, x_recv, xs, xr))
    outer_forward(x_recv)

    @pl.loop(0, entries // group)
    def _(g):
        ks = [g * group + j for j in range(group)]
        signals = [table_product(fh[k], fl[k], work[k]) for k in ks]
        products = []
        for k, x in zip(ks, signals):
            h = spectrum[k]
            xre, xim, hre, him = x[:INNER], x[INNER:], h[:INNER], h[INNER:]
            products.append(jnp.concatenate([xre * hre - xim * him, xre * him + xim * hre], axis=0))
        made = [table_product(ih[k], il[k], product) for k, product in zip(ks, products)]
        for k, value in zip(ks, made):
            work[k] = value

    sent_all((h_send, h_recv, hs, hr))
    scale = np.float32(1.0 / (outer * INNER))
    piece = INNER // CHUNKS
    height = rows // CHUNKS

    def rows_for(ref, index, p, q):
        for j in range(2):
            value = work[2 * p + j, pl.ds(q * piece, piece), :] * scale
            ref[index, pl.ds(q * height + j * piece, piece), :] = value.astype(bf16)

    def returned(p, q, source):
        part = pl.ds(q * height, height)
        return exchange(
            y_send.at[p, part], y_recv.at[source, part], ys.at[q * n + p], yr.at[q * n + source], {"ctx": p}
        )

    for q in range(CHUNKS):
        @pl.loop(q * (piece // 8), (q + 1) * (piece // 8))
        def _(t):
            begin = pl.multiple_of(t * 8, 8)
            near, far = pl.ds(begin, 8), pl.ds(INNER + begin, 8)
            bins = [(work[k, near, :], work[k, far, :] if 0 < k < half else None) for k in range(entries)]
            for j, value in enumerate(inverse_real(bins, outer)):
                work[j, near, :] = value

        @each_peer
        def _(p):
            rows_for(y_send, p, p, q)
            returned(p, q, me).start()

        rows_for(y_recv, me, me, q)

    def gate(p, q):
        lanes = lanes_of(p)
        for j in range(2):
            there, here = pl.ds(j * INNER + q * piece, piece), pl.ds(q * height + j * piece, piece)
            sum_of = y_recv[p, here, :].astype(f32) + direct[there, lanes]
            gated[here, lanes] = (queries[there, lanes] * sum_of).astype(bf16)

    def partial_copy(i):
        return exchange(p_send.at[i], p_recv.at[i], ps.at[i], pr.at[i], {"chan": other})

    for q in range(CHUNKS):
        gate(me, q)

        @each_peer
        def _(p):
            returned(p, q, p).wait_recv()
            gate(p, q)

        @pl.loop(q * tiles, (q + 1) * tiles)
        def _(i):
            weight_copy(i).wait()
            left = gated[pl.ds(q * height, height), :]
            part = jnp.dot(left, weights[lax.rem(i, 2)], preferred_element_type=f32)
            p_send[i] = part.astype(bf16)
            partial_copy(i).start()
            weight_copy(i + 2).start()

    @pl.loop(0, tiles)
    def _(i):
        number = i + CHUNKS * tiles
        weight_copy(number).wait()
        own = jnp.dot(gated[...], weights[lax.rem(number, 2)], preferred_element_type=f32)

        @pl.when(i + 2 < tiles)
        def _():
            weight_copy(number + 2).start()

        columns = pl.ds(pl.multiple_of(i * TILE, TILE), TILE)
        for q in range(CHUNKS):
            partial_copy(q * tiles + i).wait_recv()
            for j in range(2):
                begin = q * height + j * piece
                came = p_recv[q * tiles + i, pl.ds(j * piece, piece), :].astype(f32)
                out[pl.ds(j * INNER + q * piece, piece), columns] = (own[begin : begin + piece] + came).astype(bf16)

    sent_all((x_send, x_recv, xs, xr))
    for q in range(CHUNKS):
        @each_peer
        def _(p):
            returned(p, q, me).wait_send()

    for tail in tails:
        tail.wait_send()

    @pl.loop(0, CHUNKS * tiles)
    def _(i):
        partial_copy(i).wait_send()


def fused_local(raw_query, raw_key, raw_value, short_filter, long_filter, skip, w_out):
    n = lax.axis_size("ctx")
    rows, width = raw_query.shape
    features = w_out.shape[1] // 2
    outer = 4 * n
    tiles = features // TILE
    entries = outer // 2 + 1
    table = inner_tables(outer, INNER)
    bf16, f32 = jnp.bfloat16, jnp.float32

    def parts_of(values):
        high = values.astype(bf16)
        low = (values - high.astype(np.float32)).astype(bf16)
        return jnp.asarray(high), jnp.asarray(low)

    fh, fl = parts_of(table)
    ih, il = parts_of(np.ascontiguousarray(table.transpose(0, 2, 1)))
    anywhere = pl.BlockSpec(memory_space=pl.ANY)
    inside = pl.BlockSpec(memory_space=pltpu.VMEM)
    tables = pltpu.VMEM((entries, 2 * INNER, 2 * INNER), bf16)
    blocks = pltpu.VMEM((n, rows, LANES), bf16)
    bins = pltpu.VMEM((entries, 2 * INNER, LANES), f32)
    dma = pltpu.SemaphoreType.DMA
    return pl.pallas_call(
        functools.partial(whole_kernel, n),
        out_shape=jax.ShapeDtypeStruct((rows, features), bf16),
        in_specs=[anywhere] * 3 + [inside, anywhere, inside] + [anywhere] * 5,
        out_specs=inside,
        scratch_shapes=[
            pltpu.VMEM((3, rows, width), bf16),
            pltpu.VMEM((rows, width), f32),
            tables, tables, tables, tables,
            pltpu.VMEM((3, 16, width), bf16),
            blocks, blocks, blocks, blocks, blocks,
            pltpu.VMEM((rows, width), f32),
            pltpu.VMEM((rows, width), f32),
            bins, bins,
            pltpu.VMEM((rows, width), bf16),
            pltpu.VMEM((2, width, TILE), bf16),
            pltpu.VMEM((CHUNKS * tiles, rows // CHUNKS, TILE), bf16),
            pltpu.VMEM((CHUNKS * tiles, rows // CHUNKS, TILE), bf16),
            dma((8,)), dma((2,)), dma((3,)), dma((3,)),
            dma((n,)), dma((n,)), dma((n,)), dma((n,)), dma((CHUNKS * n,)), dma((CHUNKS * n,)),
            dma((CHUNKS * tiles,)), dma((CHUNKS * tiles,)),
        ],
        compiler_params=pltpu.CompilerParams(
            collective_id=0, has_side_effects=True, vmem_limit_bytes=60 * 1024 * 1024
        ),
    )(
        raw_query, raw_key, raw_value, short_filter, long_filter,
        skip.reshape(1, width), w_out, fh, fl, ih, il,
    )


def local(*arrays):
    rows, width = arrays[0].shape
    n = lax.axis_size("ctx")
    fits = lax.axis_size("chan") == 2 and rows == 2 * INNER and width == n * LANES
    fits = fits and n & (n - 1) == 0 and n <= 16 and arrays[6].shape[1] % (4 * TILE) == 0
    return fused_local(*arrays) if fits else plain_local(*arrays)


def solution(mesh):
    in_specs = (
        P("ctx", "chan"),
        P("ctx", "chan"),
        P("ctx", "chan"),
        P(None, None, "chan"),
        P("ctx", "chan"),
        P("chan"),
        P("chan", None),
    )
    out_specs = P("ctx", "chan")
    return jax.shard_map(local, mesh=mesh, in_specs=in_specs, out_specs=out_specs, check_vma=False)
```
